32 devices in a mesh: face: 4 (over y, core), tile: 8 (over z, x).
Axes of the slice: x: 2, y: 2, z: 4, core: 2. Of those that a mesh axis runs over, the one named last changes fastest.
Arguments:
- field: bfloat16 [4, 128, 256, 256], P('face', None, 'tile'), may hold values from -6 to 6
- conv_weight: bfloat16 [9, 256, 256], replicated, may hold values from -0.125 to 0.125
- norm_gain: float32 [256], replicated, may hold values from 0.5 to 1.5
- filter_gain: float32 [2, 256], replicated, may hold values from -1 to 1
- seam_face: int32 [4, 2], replicated, may hold values from 0 to 3
- seam_code: int32 [4, 2], replicated, may hold values from 0 to 3
Outputs:
- filtered: bfloat16 [4, 128, 256, 256], P('face', None, 'tile')
The draws below stay inside these ranges and needn't reach their ends.
All inputs are finite; a program needn't handle non-finite values.
Results may differ from the reference program's by a relative error of at most 0.0056.
Values may be sent and summed in bfloat16 or wider, within the bound.
A program may use at most 128 MiB of HBM per device.

```python
import jax
import jax.numpy as jnp
from jax import lax

C = 256
ROWS = 128
FACES = 4
W = 256
L = 1024
MODES = 256


def place_ends(drawn, own_key, least, high):
    dims = drawn.shape
    place = [jax.random.randint(jax.random.fold_in(own_key, axis), (), 0, dims[axis]) for axis in range(len(dims))]
    drawn = drawn.at[tuple(place)].set(least)
    longest = dims.index(max(dims))
    place[longest] = (place[longest] + 1) % dims[longest]
    return drawn.at[tuple(place)].set(high)


def level_of(own_key, dims, pieces, smallest, largest):
    factor_of = 1.0
    for dim, parts in pieces:
        draws = jax.random.uniform(jax.random.fold_in(jax.random.fold_in(own_key, 6), dim), (parts,), jnp.float32, smallest / len(pieces), largest / len(pieces))
        factor_of = factor_of * jnp.repeat(jnp.exp(draws), dims[dim] // parts).reshape((-1,) + (1,) * (len(dims) - 1 - dim))
    return factor_of


def normal_values(stream_key, shape, scale, most, shards=(), kind=jnp.bfloat16):
    drawn = jax.random.normal(stream_key, shape, jnp.float32) * scale
    if len(shards) > 0:
        drawn = level_of(stream_key, shape, shards, -0.22, 0.18) * drawn
    return jnp.clip(drawn, min=-most, max=most).astype(kind)


def setup_inputs(seed: int = 0) -> dict:
    key_of = jax.random.split(jax.random.key(seed), 7)
    return {
        "field": normal_values(key_of[0], (FACES, ROWS, W, C), 1.0, 6.0, ((0, 4), (2, 8))),
        "conv_weight": normal_values(key_of[1], (9, C, C), (9 * C) ** -0.5, 0.125),
        "norm_gain": jnp.clip(1.0 + 0.1 * jax.random.normal(key_of[2], (C,), jnp.float32), 0.5, 1.5),
        "filter_gain": jnp.clip(jax.random.uniform(key_of[3], (2, MODES), jnp.float32, -1.0, 1.0), -1.0, 1.0),
        "seam_face": place_ends(jax.random.randint(key_of[4], (FACES, 2), 0, FACES), jax.random.fold_in(key_of[4], 1), 0, FACES - 1).astype(jnp.int32),
        "seam_code": place_ends(jax.random.randint(key_of[5], (FACES, 2), 0, 4), jax.random.fold_in(key_of[5], 1), 0, 3).astype(jnp.int32),
    }


def seam_column(field, source, code):
    column = jnp.where(code % 2 == 0, 0, W - 1)
    strip = field[source, :, column, :]
    return jnp.where(code >= 2, strip[::-1], strip)

def make_table():
    places = jnp.arange(L, dtype=jnp.int32)
    waves = jnp.arange(MODES, dtype=jnp.int32)
    phase = places[:, None] * waves[None, :] % L
    angle = phase.astype(jnp.float32) * (2.0 * jnp.pi / L)
    return jnp.concatenate([jnp.cos(angle), jnp.sin(angle)], axis=1).astype(jnp.bfloat16)

def reference(field, conv_weight, norm_gain, filter_gain, seam_face, seam_code):
    lefts = jnp.stack([seam_column(field, seam_face[f, 0], seam_code[f, 0]) for f in range(FACES)])
    rights = jnp.stack([seam_column(field, seam_face[f, 1], seam_code[f, 1]) for f in range(FACES)])
    framed = jnp.concatenate([lefts[:, :, None, :], field, rights[:, :, None, :]], axis=2)
    framed = jnp.pad(framed, ((0, 0), (1, 1), (0, 0), (0, 0)))
    weights = conv_weight.astype(jnp.float32)

    def one_face(frame):
        total = jnp.zeros((ROWS * W, C), jnp.float32)
        for tap in range(9):
            row_off, col_off = (tap // 3, tap % 3)
            window = frame[row_off:row_off + ROWS, col_off:col_off + W, :].astype(jnp.float32)
            total = total + jnp.dot(window.reshape(ROWS * W, C), weights[tap])
        centered = total - lax.optimization_barrier(jnp.mean(total, axis=1, keepdims=True))
        variance = lax.optimization_barrier(jnp.mean(centered * centered, axis=1, keepdims=True))
        normed = centered / jnp.sqrt(variance + 1e-05) * norm_gain
        return jax.nn.gelu(normed).reshape(ROWS, W, C)
    branch = lax.map(one_face, framed)
    mixed = (field.astype(jnp.float32) + branch).astype(jnp.bfloat16)
    cycles = jnp.transpose(mixed, (1, 0, 2, 3)).reshape(ROWS, L, C)
    table = make_table().astype(jnp.float32)
    waves = jnp.arange(MODES, dtype=jnp.int32)
    scale = (jnp.where(waves == 0, 1.0, 2.0) / L).astype(jnp.float32)[:, None]
    real_gain = filter_gain[0][:, None]
    imag_gain = filter_gain[1][:, None]

    def one_cycle(cycle):
        values = cycle.astype(jnp.float32)
        coeffs = jnp.dot(table.T, values, precision=lax.Precision.HIGHEST)
        cos_part, sin_part = (coeffs[:MODES], coeffs[MODES:])
        held_real = ((real_gain * cos_part + imag_gain * sin_part) * scale).astype(jnp.bfloat16)
        held_imag = ((imag_gain * cos_part - real_gain * sin_part) * scale).astype(jnp.bfloat16)
        stacked = jnp.concatenate([held_real, -held_imag], axis=0).astype(jnp.float32)
        correction = jnp.dot(table, stacked, precision=lax.Precision.HIGHEST)
        return (values + correction).astype(jnp.bfloat16)
    out = lax.map(one_cycle, cycles)
    return jnp.transpose(out.reshape(ROWS, FACES, W, C), (1, 0, 2, 3))
```

```python
import functools

import jax
import jax.numpy as jnp
import numpy as np
from jax import lax
from jax.experimental import pallas as pl
from jax.experimental.pallas import tpu as pltpu
from jax.sharding import PartitionSpec as P

MESH = pl.DeviceIdType.MESH
BF = jnp.bfloat16
F32 = jnp.float32


def make_table(length, modes):
    phase = np.arange(length)[:, None] * np.arange(modes)[None, :] % length
    angle = phase.astype(np.float64) * (2.0 * np.pi / length)
    return np.concatenate([np.cos(angle), np.sin(angle)], axis=1).astype(BF)


def kernel(
    faces,
    tiles,
    x_ref,
    edge_ref,
    w_ref,
    gain_ref,
    fgain_ref,
    table_ref,
    tablet_ref,
    sface_ref,
    scode_ref,
    out_ref,
    seam,
    near,
    halo,
    x3,
    mixed,
    cyc,
    near_send,
    near_recv,
    seam_send,
    seam_recv,
    send1,
    recv1,
    send2,
    recv2,
    self_sem,
):
    rows, width, chan = x_ref.shape
    devices = faces * tiles
    owned = rows // devices
    phases, part = cyc.shape[0], cyc.shape[1]
    length = devices * width
    modes = fgain_ref.shape[1]
    half = tiles // 2
    group = half * owned
    face = lax.axis_index("face")
    tile = lax.axis_index("tile")
    me = face * tiles + tile

    barrier = pltpu.get_barrier_semaphore()

    def peer(k):
        side = k // (faces * half)
        rest = k % (faces * half)
        pf = (face + rest // half) % faces
        pt = ((tile // half + 1 + side) % 2) * half + (tile % half + rest % half) % half
        return pf, pt

    own = devices // 2

    def each_peer(fn):
        def step(k, carry):
            @pl.when(k != own)
            def _():
                pf, pt = peer(k)
                fn(pf, pt)

            return carry

        lax.fori_loop(0, devices, step, 0)

    each_peer(
        lambda pf, pt: pl.semaphore_signal(barrier, inc=1, device_id=(pf, pt), device_id_type=MESH)
    )
    pl.semaphore_wait(barrier, devices - 1)

    def to_right():
        return pltpu.make_async_remote_copy(
            edge_ref.at[1], near.at[0], near_send.at[0], near_recv.at[0],
            device_id=(face, (tile + 1) % tiles), device_id_type=MESH,
        )

    def to_left():
        return pltpu.make_async_remote_copy(
            edge_ref.at[0], near.at[1], near_send.at[1], near_recv.at[1],
            device_id=(face, (tile + tiles - 1) % tiles), device_id_type=MESH,
        )

    def seam_copy(slot, side, k):
        pf = (face + k // 2) % faces
        pt = (tile + (k % 2) * (tiles - 1)) % tiles if side == 0 else (tile + (k % 2)) % tiles
        return pltpu.make_async_remote_copy(
            edge_ref.at[side], seam.at[slot], seam_send.at[k], seam_recv.at[slot],
            device_id=(pf, pt), device_id_type=MESH,
        )

    def seam_local(side):
        return pltpu.make_async_copy(edge_ref.at[side], seam.at[face * 2 + side], seam_recv.at[face * 2 + side])

    for side, end in ((0, 0), (1, tiles - 1)):
        @pl.when(tile == end)
        def _():
            for k in range(1, 2 * faces):
                seam_copy(face * 2 + side, side, k).start()
            seam_local(side).start()

    @pl.when(tile < tiles - 1)
    def _():
        to_right().start()

    @pl.when(tile > 0)
    def _():
        to_left().start()

    x3[0] = jnp.zeros(x3.shape[1:], BF)
    x3[rows + 1] = jnp.zeros(x3.shape[1:], BF)

    @pl.when(tile > 0)
    def _():
        to_right().wait_recv()
        halo[0] = near[0].astype(F32).reshape(rows, 1, chan)

    @pl.when(tile < tiles - 1)
    def _():
        to_left().wait_recv()
        halo[1] = near[1].astype(F32).reshape(rows, 1, chan)

    down = lax.broadcasted_iota(jnp.int32, (rows, rows), 0)
    across = lax.broadcasted_iota(jnp.int32, (rows, rows), 1)
    for side, end in ((0, 0), (1, tiles - 1)):
        @pl.when(tile == end)
        def _():
            for slot in range(2 * faces):
                pltpu.make_async_copy(edge_ref.at[0], seam.at[slot], seam_recv.at[slot]).wait()
            code = scode_ref[face, side]
            strip = seam[sface_ref[face, side] * 2 + code % 2]
            target = jnp.where(code >= 2, rows - 1 - down, down)
            order = jnp.where(target == across, 1.0, 0.0).astype(BF)
            halo[side] = jnp.dot(order, strip, preferred_element_type=F32).reshape(rows, 1, chan)

    batch = 8

    def shift(b, carry):
        at = pl.ds(b * batch, batch)
        dst = pl.ds(b * batch + 1, batch)
        here = x_ref[at]
        wide = here.astype(F32)
        col = lax.broadcasted_iota(jnp.int32, wide.shape, 1)
        x3[dst, :, 0:chan] = jnp.where(col == 0, halo[0, at], pltpu.roll(wide, 1, 1)).astype(BF)
        x3[dst, :, chan : 2 * chan] = here
        x3[dst, :, 2 * chan : 3 * chan] = jnp.where(
            col == width - 1, halo[1, at], pltpu.roll(wide, width - 1, 1)
        ).astype(BF)
        return carry

    lax.fori_loop(0, rows // batch, shift, 0)

    def forward(p, pf, pt):
        d = pf * tiles + pt
        return pltpu.make_async_remote_copy(
            mixed.at[pl.ds(d * owned + p * part, part)],
            cyc.at[p, :, pl.ds(me * width, width), :],
            send1.at[p, d],
            recv1.at[p, me],
            device_id=(pf, pt),
            device_id_type=MESH,
        )

    def forward_wait(p, pf, pt):
        s = pf * tiles + pt
        return pltpu.make_async_remote_copy(
            mixed.at[pl.ds(s * owned + p * part, part)],
            cyc.at[p, :, pl.ds(s * width, width), :],
            send1.at[p, s],
            recv1.at[p, s],
            device_id=(pf, pt),
            device_id_type=MESH,
        )

    def forward_self(p):
        return pltpu.make_async_copy(
            mixed.at[pl.ds(me * owned + p * part, part)],
            cyc.at[p, :, pl.ds(me * width, width), :],
            self_sem.at[0, p],
        )

    gain = gain_ref[...]

    def block(g, carry):
        side = g // faces
        pf = (face + g % faces) % faces
        ph = (tile // half + 1 + side) % 2
        base = (pf * tiles + ph * half) * owned
        total = jnp.zeros((group * width, chan), F32)
        for dy in range(3):
            total += jnp.dot(
                x3[pl.ds(base + dy, group)].reshape(group * width, 3 * chan),
                w_ref[dy],
                preferred_element_type=F32,
            )
        step = group // 4 if group % 4 == 0 else group
        for q in range(group // step):
            piece = total[q * step * width : (q + 1) * step * width]
            centered = piece - jnp.mean(piece, axis=1, keepdims=True)
            variance = jnp.mean(centered * centered, axis=1, keepdims=True)
            normed = centered * (lax.rsqrt(variance + 1e-05)) * gain
            inner = normed * (0.7978845608028654 + 0.035677408136300125 * (normed * normed))
            act = 0.5 * normed * (1.0 + jnp.tanh(inner))
            src = x_ref[pl.ds(base + q * step, step)].astype(F32)
            mixed[pl.ds(base + q * step, step)] = (src + act.reshape(step, width, chan)).astype(BF)

        def push(i, inner_carry):
            pt = ph * half + (tile % half + i) % half

            @pl.when(g * half + i != own)
            def _():
                forward(0, pf, pt).start()

            return inner_carry

        lax.fori_loop(0, half, push, 0)
        return carry

    lax.fori_loop(0, 2 * faces, block, 0)
    for p in range(phases):
        forward_self(p).start()
    for p in range(1, phases):
        each_peer(lambda pf, pt: forward(p, pf, pt).start())

    def back(p, pf, pt):
        d = pf * tiles + pt
        return pltpu.make_async_remote_copy(
            cyc.at[p, :, pl.ds(d * width, width), :],
            out_ref.at[pl.ds(me * owned + p * part, part)],
            send2.at[p, d],
            recv2.at[p, me],
            device_id=(pf, pt),
            device_id_type=MESH,
        )

    def back_wait(p, pf, pt):
        s = pf * tiles + pt
        return pltpu.make_async_remote_copy(
            cyc.at[p, :, pl.ds(s * width, width), :],
            out_ref.at[pl.ds(s * owned + p * part, part)],
            send2.at[p, s],
            recv2.at[p, s],
            device_id=(pf, pt),
            device_id_type=MESH,
        )

    def back_self(p):
        return pltpu.make_async_copy(
            cyc.at[p, :, pl.ds(me * width, width), :],
            out_ref.at[pl.ds(me * owned + p * part, part)],
            self_sem.at[1, p],
        )

    width_m = min(modes, 256)
    eye = lax.broadcasted_iota(jnp.int32, (width_m, width_m), 0) == lax.broadcasted_iota(
        jnp.int32, (width_m, width_m), 1
    )
    stand = lambda row: jnp.sum(jnp.where(eye, row, 0.0), axis=1, keepdims=True)

    def filter_row(p, r):
        held = []
        for start in range(0, modes, width_m):
            waves = start + lax.broadcasted_iota(jnp.int32, (width_m, 1), 0)
            scale = jnp.where(waves == 0, 1.0 / length, 2.0 / length)
            real_gain = stand(fgain_ref[0:1, start : start + width_m]) * scale
            imag_gain = stand(fgain_ref[1:2, start : start + width_m]) * scale
            line = cyc[p, r]
            cos_part = jnp.dot(tablet_ref[start : start + width_m], line, preferred_element_type=F32)
            sin_part = jnp.dot(
                tablet_ref[modes + start : modes + start + width_m], line, preferred_element_type=F32
            )
            held.append(
                (
                    (real_gain * cos_part + imag_gain * sin_part).astype(BF),
                    (real_gain * sin_part - imag_gain * cos_part).astype(BF),
                )
            )
        stacked = jnp.concatenate([h[0] for h in held] + [h[1] for h in held], axis=0)
        piece = 256

        def add(b, carry):
            at = pl.ds(pl.multiple_of(b * piece, piece), piece)
            fix = jnp.dot(table_ref[at], stacked, preferred_element_type=F32)
            cyc[p, r, at] = (cyc[p, r, at].astype(F32) + fix).astype(BF)
            return carry

        lax.fori_loop(0, length // piece, add, 0)

    for p in range(phases):
        each_peer(lambda pf, pt: forward_wait(p, pf, pt).wait_recv())
        forward_self(p).wait()

        def one(r, carry):
            filter_row(p, r)
            return carry

        lax.fori_loop(0, part, one, 0)
        each_peer(lambda pf, pt: back(p, pf, pt).start())
        back_self(p).start()

    @pl.when(tile < tiles - 1)
    def _():
        to_right().wait_send()

    @pl.when(tile > 0)
    def _():
        to_left().wait_send()

    for side, end in ((0, 0), (1, tiles - 1)):
        @pl.when(tile == end)
        def _():
            for k in range(1, 2 * faces):
                seam_copy(face * 2 + side, side, k).wait_send()

    for p in range(phases):
        each_peer(lambda pf, pt: forward(p, pf, pt).wait_send())
    for p in range(phases):
        each_peer(lambda pf, pt: back_wait(p, pf, pt).wait_recv())
        each_peer(lambda pf, pt: back(p, pf, pt).wait_send())
        back_self(p).wait()


def per_device(faces, tiles, field, conv_weight, norm_gain, filter_gain, seam_face, seam_code):
    block_in = field[0]
    rows, width, chan = block_in.shape
    modes = filter_gain.shape[1]
    devices = faces * tiles
    length = devices * width
    owned = rows // devices
    phases = 2 if owned % 2 == 0 else 1
    part = owned // phases
    table = make_table(length, modes)
    edges = jnp.stack([block_in[:, 0], block_in[:, -1]])
    vmem = pl.BlockSpec(memory_space=pltpu.VMEM)
    smem = pl.BlockSpec(memory_space=pltpu.SMEM)
    dma = pltpu.SemaphoreType.DMA
    out = pl.pallas_call(
        functools.partial(kernel, faces, tiles),
        out_shape=jax.ShapeDtypeStruct((rows, width, chan), BF),
        in_specs=[vmem] * 7 + [smem] * 2,
        out_specs=vmem,
        scratch_shapes=[
            pltpu.VMEM((2 * faces, rows, chan), BF),
            pltpu.VMEM((2, rows, chan), BF),
            pltpu.VMEM((2, rows, 1, chan), F32),
            pltpu.VMEM((rows + 2, width, 3 * chan), BF),
            pltpu.VMEM((rows, width, chan), BF),
            pltpu.VMEM((phases, part, length, chan), BF),
            dma((2,)),
            dma((2,)),
            dma((2 * faces,)),
            dma((2 * faces,)),
            dma((phases, devices)),
            dma((phases, devices)),
            dma((phases, devices)),
            dma((phases, devices)),
            dma((2, phases)),
        ],
        compiler_params=pltpu.CompilerParams(
            collective_id=0, has_side_effects=True, vmem_limit_bytes=60 * 1024 * 1024
        ),
    )(
        block_in,
        edges,
        conv_weight.reshape(3, 3 * chan, chan),
        norm_gain.reshape(1, chan),
        filter_gain,
        jnp.asarray(table),
        jnp.asarray(np.ascontiguousarray(table.T)),
        seam_face,
        seam_code,
    )
    return out[None]


def solution(mesh):
    placed = (P("face", None, "tile", None), P(), P(), P(), P(), P())
    return jax.shard_map(
        functools.partial(per_device, mesh.shape["face"], mesh.shape["tile"]),
        mesh=mesh,
        in_specs=placed,
        out_specs=P("face", None, "tile", None),
        check_vma=False,
    )
```

```python
import functools

import jax
import jax.numpy as jnp
import numpy as np
from jax import lax
from jax.experimental import pallas as pl
from jax.experimental.pallas import tpu as pltpu
from jax.sharding import PartitionSpec as P

MESH = pl.DeviceIdType.MESH
BF = jnp.bfloat16
F32 = jnp.float32


def make_table(length, modes):
    phase = np.arange(length)[:, None] * np.arange(modes)[None, :] % length
    angle = phase.astype(np.float64) * (2.0 * np.pi / length)
    return np.concatenate([np.cos(angle), np.sin(angle)], axis=1).astype(BF)


def kernel(
    faces,
    tiles,
    x_ref,
    gain_ref,
    fgain_ref,
    w_hbm,
    table_hbm,
    tablet_hbm,
    sface_ref,
    scode_ref,
    out_ref,
    w_ref,
    table_ref,
    tablet_ref,
    edge_ref,
    seam,
    near,
    halo,
    x3,
    mixed,
    cyc,
    near_send,
    near_recv,
    seam_send,
    seam_recv,
    send1,
    recv1,
    send2,
    recv2,
    self_sem,
    load_sem,
):
    rows, width, chan = x_ref.shape
    devices = faces * tiles
    owned = rows // devices
    phases, part = cyc.shape[0], cyc.shape[1]
    length = devices * width
    modes = fgain_ref.shape[1]
    half = tiles // 2
    group = half * owned
    face = lax.axis_index("face")
    tile = lax.axis_index("tile")
    me = face * tiles + tile

    barrier = pltpu.get_barrier_semaphore()

    def peer(k):
        side = k // (faces * half)
        rest = k % (faces * half)
        pf = (face + rest // half) % faces
        pt = ((tile // half + 1 + side) % 2) * half + (tile % half + rest % half) % half
        return pf, pt

    own = devices // 2

    def each_peer(fn):
        def step(k, carry):
            @pl.when(k != own)
            def _():
                pf, pt = peer(k)
                fn(pf, pt)

            return carry

        lax.fori_loop(0, devices, step, 0)

    each_peer(
        lambda pf, pt: pl.semaphore_signal(barrier, inc=1, device_id=(pf, pt), device_id_type=MESH)
    )
    loads = [
        pltpu.make_async_copy(src, dst, load_sem.at[k])
        for k, (src, dst) in enumerate(
            ((w_hbm, w_ref), (tablet_hbm, tablet_ref), (table_hbm, table_ref))
        )
    ]
    for load in loads:
        load.start()

    def pick(b, carry):
        at = pl.ds(b * 16, 16)
        edge_ref[0, at] = x_ref[at].astype(F32)[:, 0, :].astype(BF)
        edge_ref[1, at] = x_ref[at].astype(F32)[:, width - 1, :].astype(BF)
        return carry

    lax.fori_loop(0, rows // 16, pick, 0)
    pl.semaphore_wait(barrier, devices - 1)

    def to_right():
        return pltpu.make_async_remote_copy(
            edge_ref.at[1], near.at[0], near_send.at[0], near_recv.at[0],
            device_id=(face, (tile + 1) % tiles), device_id_type=MESH,
        )

    def to_left():
        return pltpu.make_async_remote_copy(
            edge_ref.at[0], near.at[1], near_send.at[1], near_recv.at[1],
            device_id=(face, (tile + tiles - 1) % tiles), device_id_type=MESH,
        )

    def seam_copy(slot, k, pf, pt):
        return pltpu.make_async_remote_copy(
            seam.at[slot], seam.at[slot], seam_send.at[k], seam_recv.at[slot],
            device_id=(pf, pt), device_id_type=MESH,
        )

    ends = ((0, 0, tiles - 1), (1, tiles - 1, 0))

    @pl.when(tile < tiles - 1)
    def _():
        to_right().start()

    @pl.when(tile > 0)
    def _():
        to_left().start()

    for side, end, other in ends:
        @pl.when(tile == end)
        def _():
            mine = face * 2 + side
            seam[mine] = edge_ref[side]
            seam_copy(mine, 0, face, other).start()
            for k in range(1, faces):
                seam_copy(mine, k, (face + k) % faces, end).start()

    @pl.when(tile > 0)
    def _():
        to_right().wait_recv()
        halo[0] = near[0].astype(F32).reshape(rows, 1, chan)

    @pl.when(tile < tiles - 1)
    def _():
        to_left().wait_recv()
        halo[1] = near[1].astype(F32).reshape(rows, 1, chan)

    down = lax.broadcasted_iota(jnp.int32, (rows, rows), 0)
    across = lax.broadcasted_iota(jnp.int32, (rows, rows), 1)
    for side, end, other in ends:
        @pl.when(tile == end)
        def _():
            far = face * 2 + 1 - side
            seam_copy(far, 0, face, other).wait_recv()
            for k in range(1, faces):
                seam_copy(far, faces + k - 1, (face + k) % faces, end).start()
            for k in range(1, faces):
                pf = (face + k) % faces
                seam_copy(pf * 2 + side, k, pf, end).wait_recv()
                seam_copy(pf * 2 + 1 - side, faces + k - 1, pf, end).wait_recv()
            code = scode_ref[side, face]
            strip = seam[sface_ref[side, face] * 2 + code % 2]
            target = jnp.where(code >= 2, rows - 1 - down, down)
            order = jnp.where(target == across, 1.0, 0.0).astype(BF)
            halo[side] = jnp.dot(order, strip, preferred_element_type=F32).reshape(rows, 1, chan)

    def shift(dst, row, count):
        at = pl.ds(row, count)
        here = x_ref[at]
        wide = here.astype(F32)
        col = lax.broadcasted_iota(jnp.int32, wide.shape, 1)
        x3[dst, :, 0:chan] = jnp.where(col == 0, halo[0, at], pltpu.roll(wide, 1, 1)).astype(BF)
        x3[dst, :, chan : 2 * chan] = here
        x3[dst, :, 2 * chan : 3 * chan] = jnp.where(
            col == width - 1, halo[1, at], pltpu.roll(wide, width - 1, 1)
        ).astype(BF)

    def frame(base):
        batch = 8 if group % 8 == 0 else group
        for b in range(0, group, batch):
            shift(pl.ds(b + 1, batch), base + b, batch)
        for dst, row, edge in ((0, base - 1, 0), (group + 1, base + group, rows - group)):
            @pl.when(base != edge)
            def _():
                shift(pl.ds(dst, 1), row, 1)

            @pl.when(base == edge)
            def _():
                x3[dst] = jnp.zeros(x3.shape[1:], BF)

    loads[0].wait()

    def forward(p, pf, pt):
        d = pf * tiles + pt
        return pltpu.make_async_remote_copy(
            mixed.at[pl.ds(d * owned + p * part, part)],
            cyc.at[p, :, pl.ds(me * width, width), :],
            send1.at[p, d],
            recv1.at[p, me],
            device_id=(pf, pt),
            device_id_type=MESH,
        )

    def forward_wait(p, pf, pt):
        s = pf * tiles + pt
        return pltpu.make_async_remote_copy(
            mixed.at[pl.ds(s * owned + p * part, part)],
            cyc.at[p, :, pl.ds(s * width, width), :],
            send1.at[p, s],
            recv1.at[p, s],
            device_id=(pf, pt),
            device_id_type=MESH,
        )

    def forward_self(p):
        return pltpu.make_async_copy(
            mixed.at[pl.ds(me * owned + p * part, part)],
            cyc.at[p, :, pl.ds(me * width, width), :],
            self_sem.at[0, p],
        )

    gain = gain_ref[...]

    def block(g, carry):
        side = g // faces
        pf = (face + g % faces) % faces
        ph = (tile // half + 1 + side) % 2
        base = (pf * tiles + ph * half) * owned
        frame(base)
        total = jnp.zeros((group * width, chan), F32)
        for dy in range(3):
            total += jnp.dot(
                x3[pl.ds(dy, group)].reshape(group * width, 3 * chan),
                w_ref[dy],
                preferred_element_type=F32,
            )
        step = group // 4 if group % 4 == 0 else group
        for q in range(group // step):
            piece = total[q * step * width : (q + 1) * step * width]
            centered = piece - jnp.mean(piece, axis=1, keepdims=True)
            variance = jnp.mean(centered * centered, axis=1, keepdims=True)
            normed = centered * (lax.rsqrt(variance + 1e-05)) * gain
            inner = normed * (0.7978845608028654 + 0.035677408136300125 * (normed * normed))
            act = 0.5 * normed * (1.0 + jnp.tanh(inner))
            src = x_ref[pl.ds(base + q * step, step)].astype(F32)
            mixed[pl.ds(base + q * step, step)] = (src + act.reshape(step, width, chan)).astype(BF)

        def push(i, inner_carry):
            pt = ph * half + (tile % half + i) % half

            @pl.when(g * half + i != own)
            def _():
                forward(0, pf, pt).start()

            return inner_carry

        lax.fori_loop(0, half, push, 0)
        return carry

    lax.fori_loop(0, 2 * faces, block, 0)
    for p in range(phases):
        forward_self(p).start()
    for p in range(1, phases):
        each_peer(lambda pf, pt: forward(p, pf, pt).start())

    def back(p, pf, pt):
        d = pf * tiles + pt
        return pltpu.make_async_remote_copy(
            cyc.at[p, :, pl.ds(d * width, width), :],
            out_ref.at[pl.ds(me * owned + p * part, part)],
            send2.at[p, d],
            recv2.at[p, me],
            device_id=(pf, pt),
            device_id_type=MESH,
        )

    def back_wait(p, pf, pt):
        s = pf * tiles + pt
        return pltpu.make_async_remote_copy(
            cyc.at[p, :, pl.ds(s * width, width), :],
            out_ref.at[pl.ds(s * owned + p * part, part)],
            send2.at[p, s],
            recv2.at[p, s],
            device_id=(pf, pt),
            device_id_type=MESH,
        )

    def back_self(p):
        return pltpu.make_async_copy(
            cyc.at[p, :, pl.ds(me * width, width), :],
            out_ref.at[pl.ds(me * owned + p * part, part)],
            self_sem.at[1, p],
        )

    loads[1].wait()
    loads[2].wait()
    width_m = min(modes, 256)
    eye = lax.broadcasted_iota(jnp.int32, (width_m, width_m), 0) == lax.broadcasted_iota(
        jnp.int32, (width_m, width_m), 1
    )
    stand = lambda row: jnp.sum(jnp.where(eye, row, 0.0), axis=1, keepdims=True)

    def filter_row(p, r):
        held = []
        for start in range(0, modes, width_m):
            waves = start + lax.broadcasted_iota(jnp.int32, (width_m, 1), 0)
            scale = jnp.where(waves == 0, 1.0 / length, 2.0 / length)
            real_gain = stand(fgain_ref[0:1, start : start + width_m]) * scale
            imag_gain = stand(fgain_ref[1:2, start : start + width_m]) * scale
            line = cyc[p, r]
            cos_part = jnp.dot(tablet_ref[start : start + width_m], line, preferred_element_type=F32)
            sin_part = jnp.dot(
                tablet_ref[modes + start : modes + start + width_m], line, preferred_element_type=F32
            )
            held.append(
                (
                    (real_gain * cos_part + imag_gain * sin_part).astype(BF),
                    (real_gain * sin_part - imag_gain * cos_part).astype(BF),
                )
            )
        stacked = jnp.concatenate([h[0] for h in held] + [h[1] for h in held], axis=0)
        piece = 256

        def add(b, carry):
            at = pl.ds(pl.multiple_of(b * piece, piece), piece)
            fix = jnp.dot(table_ref[at], stacked, preferred_element_type=F32)
            cyc[p, r, at] = (cyc[p, r, at].astype(F32) + fix).astype(BF)
            return carry

        lax.fori_loop(0, length // piece, add, 0)

    for p in range(phases):
        each_peer(lambda pf, pt: forward_wait(p, pf, pt).wait_recv())
        forward_self(p).wait()

        def one(r, carry):
            filter_row(p, r)
            return carry

        lax.fori_loop(0, part, one, 0)
        each_peer(lambda pf, pt: back(p, pf, pt).start())
        back_self(p).start()

    @pl.when(tile < tiles - 1)
    def _():
        to_right().wait_send()

    @pl.when(tile > 0)
    def _():
        to_left().wait_send()

    for side, end, other in ends:
        @pl.when(tile == end)
        def _():
            seam_copy(face * 2 + side, 0, face, other).wait_send()
            for k in range(1, faces):
                pf = (face + k) % faces
                seam_copy(face * 2 + side, k, pf, end).wait_send()
                seam_copy(face * 2 + 1 - side, faces + k - 1, pf, end).wait_send()

    for p in range(phases):
        each_peer(lambda pf, pt: forward(p, pf, pt).wait_send())
    for p in range(phases):
        each_peer(lambda pf, pt: back_wait(p, pf, pt).wait_recv())
        each_peer(lambda pf, pt: back(p, pf, pt).wait_send())
        back_self(p).wait()


def per_device(faces, tiles, field, conv_weight, norm_gain, filter_gain, seam_face, seam_code):
    block_in = field[0]
    rows, width, chan = block_in.shape
    modes = filter_gain.shape[1]
    devices = faces * tiles
    length = devices * width
    owned = rows // devices
    phases = 2 if owned % 2 == 0 else 1
    part = owned // phases
    table = make_table(length, modes)
    group = rows // (2 * faces)
    anyw = pl.BlockSpec(memory_space=pl.ANY)
    vmem = pl.BlockSpec(memory_space=pltpu.VMEM)
    smem = pl.BlockSpec(memory_space=pltpu.SMEM)
    dma = pltpu.SemaphoreType.DMA
    out = pl.pallas_call(
        functools.partial(kernel, faces, tiles),
        out_shape=jax.ShapeDtypeStruct((rows, width, chan), BF),
        in_specs=[vmem] * 3 + [anyw] * 3 + [smem] * 2,
        out_specs=vmem,
        scratch_shapes=[
            pltpu.VMEM((3, 3 * chan, chan), BF),
            pltpu.VMEM((length, 2 * modes), BF),
            pltpu.VMEM((2 * modes, length), BF),
            pltpu.VMEM((2, rows, chan), BF),
            pltpu.VMEM((2 * faces, rows, chan), BF),
            pltpu.VMEM((2, rows, chan), BF),
            pltpu.VMEM((2, rows, 1, chan), F32),
            pltpu.VMEM((group + 2, width, 3 * chan), BF),
            pltpu.VMEM((rows, width, chan), BF),
            pltpu.VMEM((phases, part, length, chan), BF),
            dma((2,)),
            dma((2,)),
            dma((2 * faces,)),
            dma((2 * faces,)),
            dma((phases, devices)),
            dma((phases, devices)),
            dma((phases, devices)),
            dma((phases, devices)),
            dma((2, phases)),
            dma((3,)),
        ],
        compiler_params=pltpu.CompilerParams(
            collective_id=0, has_side_effects=True, vmem_limit_bytes=60 * 1024 * 1024
        ),
    )(
        block_in,
        norm_gain.reshape(1, chan),
        filter_gain,
        conv_weight.reshape(3, 3 * chan, chan),
        jnp.asarray(table),
        jnp.asarray(np.ascontiguousarray(table.T)),
        seam_face.T,
        seam_code.T,
    )
    return out[None]


def solution(mesh):
    placed = (P("face", None, "tile", None), P(), P(), P(), P(), P())
    return jax.shard_map(
        functools.partial(per_device, mesh.shape["face"], mesh.shape["tile"]),
        mesh=mesh,
        in_specs=placed,
        out_specs=P("face", None, "tile", None),
        check_vma=False,
    )
```

```python
import functools

import jax
import jax.numpy as jnp
import numpy as np
from jax import lax
from jax.experimental import pallas as pl
from jax.experimental.pallas import tpu as pltpu
from jax.sharding import PartitionSpec as P

MESH = pl.DeviceIdType.MESH
BF = jnp.bfloat16
F32 = jnp.float32


def make_table(length, modes):
    phase = np.arange(length)[:, None] * np.arange(modes)[None, :] % length
    angle = phase.astype(np.float64) * (2.0 * np.pi / length)
    return np.concatenate([np.cos(angle), np.sin(angle)], axis=1).astype(BF)


def kernel(
    faces,
    tiles,
    x_hbm,
    gain_ref,
    fgain_ref,
    w_hbm,
    table_hbm,
    tablet_hbm,
    sface_ref,
    scode_ref,
    out_ref,
    x_ref,
    w_ref,
    table_ref,
    tablet_ref,
    edge_ref,
    seam,
    near,
    halo,
    x3,
    mixed,
    cyc,
    near_send,
    near_recv,
    seam_send,
    seam_recv,
    send1,
    recv1,
    send2,
    recv2,
    load_sem,
):
    rows, width, chan = x_hbm.shape
    devices = faces * tiles
    owned = rows // devices
    phases, part = cyc.shape[0], cyc.shape[1]
    length = devices * width
    modes = fgain_ref.shape[1]
    half = tiles // 2
    group = half * owned
    face = lax.axis_index("face")
    tile = lax.axis_index("tile")
    me = face * tiles + tile

    barrier = pltpu.get_barrier_semaphore()

    loads = [
        pltpu.make_async_copy(src, dst, load_sem.at[k])
        for k, (src, dst) in enumerate(
            ((x_hbm, x_ref), (w_hbm, w_ref), (tablet_hbm, tablet_ref), (table_hbm, table_ref))
        )
    ]
    for load in loads:
        load.start()

    def peer(k):
        side = k // (faces * half)
        rest = k % (faces * half)
        pf = (face + rest // half) % faces
        pt = ((tile // half + 1 + side) % 2) * half + (tile % half + rest % half) % half
        return pf, pt

    own = devices // 2

    def each_peer(fn):
        def step(k, carry):
            @pl.when(k != own)
            def _():
                pf, pt = peer(k)
                fn(pf, pt)

            return carry

        lax.fori_loop(0, devices, step, 0)

    each_peer(
        lambda pf, pt: pl.semaphore_signal(barrier, inc=1, device_id=(pf, pt), device_id_type=MESH)
    )
    def pick(b, carry):
        at = pl.ds(b * 16, 16)
        edge_ref[0, at] = x_ref[at, 0:16].astype(F32)[:, 0, :].astype(BF)
        edge_ref[1, at] = x_ref[at, width - 16 : width].astype(F32)[:, 15, :].astype(BF)
        return carry

    loads[0].wait()
    lax.fori_loop(0, rows // 16, pick, 0)
    pl.semaphore_wait(barrier, devices - 1)

    def to_right():
        return pltpu.make_async_remote_copy(
            edge_ref.at[1], near.at[0], near_send.at[0], near_recv.at[0],
            device_id=(face, (tile + 1) % tiles), device_id_type=MESH,
        )

    def to_left():
        return pltpu.make_async_remote_copy(
            edge_ref.at[0], near.at[1], near_send.at[1], near_recv.at[1],
            device_id=(face, (tile + tiles - 1) % tiles), device_id_type=MESH,
        )

    def seam_copy(slot, k, pf, pt):
        return pltpu.make_async_remote_copy(
            seam.at[slot], seam.at[slot], seam_send.at[k], seam_recv.at[slot],
            device_id=(pf, pt), device_id_type=MESH,
        )

    ends = ((0, 0, tiles - 1), (1, tiles - 1, 0))

    @pl.when(tile < tiles - 1)
    def _():
        to_right().start()

    @pl.when(tile > 0)
    def _():
        to_left().start()

    for side, end, other in ends:
        @pl.when(tile == end)
        def _():
            mine = face * 2 + side
            seam[mine] = edge_ref[side]
            seam_copy(mine, 0, face, other).start()
            for k in range(1, faces):
                seam_copy(mine, k, (face + k) % faces, end).start()

    @pl.when(tile > 0)
    def _():
        to_right().wait_recv()
        halo[0] = near[0].astype(F32).reshape(rows, 1, chan)

    @pl.when(tile < tiles - 1)
    def _():
        to_left().wait_recv()
        halo[1] = near[1].astype(F32).reshape(rows, 1, chan)

    down = lax.broadcasted_iota(jnp.int32, (rows, rows), 0)
    across = lax.broadcasted_iota(jnp.int32, (rows, rows), 1)
    for side, end, other in ends:
        @pl.when(tile == end)
        def _():
            far = face * 2 + 1 - side
            seam_copy(far, 0, face, other).wait_recv()
            for k in range(1, faces):
                seam_copy(far, faces + k - 1, (face + k) % faces, end).start()
            for k in range(1, faces):
                pf = (face + k) % faces
                seam_copy(pf * 2 + side, k, pf, end).wait_recv()
                seam_copy(pf * 2 + 1 - side, faces + k - 1, pf, end).wait_recv()
            code = scode_ref[side, face]
            strip = seam[sface_ref[side, face] * 2 + code % 2]
            target = jnp.where(code >= 2, rows - 1 - down, down)
            order = jnp.where(target == across, 1.0, 0.0).astype(BF)
            halo[side] = jnp.dot(order, strip, preferred_element_type=F32).reshape(rows, 1, chan)

    def shift(dst, row, count):
        at = pl.ds(row, count)
        here = x_ref[at]
        wide = here.astype(F32)
        col = lax.broadcasted_iota(jnp.int32, wide.shape, 1)
        x3[dst, :, 0:chan] = jnp.where(col == 0, halo[0, at], pltpu.roll(wide, 1, 1)).astype(BF)
        x3[dst, :, chan : 2 * chan] = here
        x3[dst, :, 2 * chan : 3 * chan] = jnp.where(
            col == width - 1, halo[1, at], pltpu.roll(wide, width - 1, 1)
        ).astype(BF)

    def frame(base):
        batch = 8 if group % 8 == 0 else group
        for b in range(0, group, batch):
            shift(pl.ds(b + 1, batch), base + b, batch)
        for dst, row, edge in ((0, base - 1, 0), (group + 1, base + group, rows - group)):
            @pl.when(base != edge)
            def _():
                shift(pl.ds(dst, 1), row, 1)

            @pl.when(base == edge)
            def _():
                x3[dst] = jnp.zeros(x3.shape[1:], BF)

    loads[1].wait()

    def forward(p, pf, pt):
        d = pf * tiles + pt
        return pltpu.make_async_remote_copy(
            mixed.at[pl.ds(d * owned + p * part, part)],
            cyc.at[p, :, pl.ds(me * width, width), :],
            send1.at[p],
            recv1.at[p],
            device_id=(pf, pt),
            device_id_type=MESH,
        )

    def forward_self(p):
        return pltpu.make_async_copy(
            mixed.at[pl.ds(me * owned + p * part, part)],
            cyc.at[p, :, pl.ds(me * width, width), :],
            recv1.at[p],
        )

    def whole(p, sem):
        return pltpu.make_async_copy(mixed.at[pl.ds(0, devices * part)], mixed.at[pl.ds(0, devices * part)], sem.at[p])

    def others(p, sem):
        return pltpu.make_async_copy(
            mixed.at[pl.ds(0, (devices - 1) * part)], mixed.at[pl.ds(0, (devices - 1) * part)], sem.at[p]
        )

    gain = gain_ref[...]

    def block(g, carry):
        side = g // faces
        pf = (face + g % faces) % faces
        ph = (tile // half + 1 + side) % 2
        base = (pf * tiles + ph * half) * owned
        frame(base)
        total = jnp.zeros((group * width, chan), F32)
        for dy in range(3):
            total += jnp.dot(
                x3[pl.ds(dy, group)].reshape(group * width, 3 * chan),
                w_ref[dy],
                preferred_element_type=F32,
            )
        step = group // 4 if group % 4 == 0 else group
        for q in range(group // step):
            piece = total[q * step * width : (q + 1) * step * width]
            centered = piece - jnp.mean(piece, axis=1, keepdims=True)
            variance = jnp.mean(centered * centered, axis=1, keepdims=True)
            normed = centered * (lax.rsqrt(variance + 1e-05)) * gain
            inner = normed * (0.7978845608028654 + 0.035677408136300125 * (normed * normed))
            act = 0.5 * normed * (1.0 + jnp.tanh(inner))
            src = x_ref[pl.ds(base + q * step, step)].astype(F32)
            mixed[pl.ds(base + q * step, step)] = (src + act.reshape(step, width, chan)).astype(BF)

        def push(i, inner_carry):
            pt = ph * half + (tile % half + i) % half

            @pl.when(g * half + i != own)
            def _():
                forward(0, pf, pt).start()

            return inner_carry

        lax.fori_loop(0, half, push, 0)
        return carry

    lax.fori_loop(0, 2 * faces, block, 0)
    for p in range(phases):
        forward_self(p).start()
    for p in range(1, phases):
        each_peer(lambda pf, pt: forward(p, pf, pt).start())

    def back(p, pf, pt):
        d = pf * tiles + pt
        return pltpu.make_async_remote_copy(
            cyc.at[p, :, pl.ds(d * width, width), :],
            out_ref.at[pl.ds(me * owned + p * part, part)],
            send2.at[p],
            recv2.at[p],
            device_id=(pf, pt),
            device_id_type=MESH,
        )

    def back_self(p):
        return pltpu.make_async_copy(
            cyc.at[p, :, pl.ds(me * width, width), :],
            out_ref.at[pl.ds(me * owned + p * part, part)],
            recv2.at[p],
        )

    loads[2].wait()
    loads[3].wait()
    width_m = min(modes, 256)
    eye = lax.broadcasted_iota(jnp.int32, (width_m, width_m), 0) == lax.broadcasted_iota(
        jnp.int32, (width_m, width_m), 1
    )
    stand = lambda row: jnp.sum(jnp.where(eye, row, 0.0), axis=1, keepdims=True)

    def filter_row(p, r):
        held = []
        for start in range(0, modes, width_m):
            waves = start + lax.broadcasted_iota(jnp.int32, (width_m, 1), 0)
            scale = jnp.where(waves == 0, 1.0 / length, 2.0 / length)
            real_gain = stand(fgain_ref[0:1, start : start + width_m]) * scale
            imag_gain = stand(fgain_ref[1:2, start : start + width_m]) * scale
            line = cyc[p, r]
            cos_part = jnp.dot(tablet_ref[start : start + width_m], line, preferred_element_type=F32)
            sin_part = jnp.dot(
                tablet_ref[modes + start : modes + start + width_m], line, preferred_element_type=F32
            )
            held.append(
                (
                    (real_gain * cos_part + imag_gain * sin_part).astype(BF),
                    (real_gain * sin_part - imag_gain * cos_part).astype(BF),
                )
            )
        stacked = jnp.concatenate([h[0] for h in held] + [h[1] for h in held], axis=0)
        piece = 256

        def add(b, carry):
            at = pl.ds(pl.multiple_of(b * piece, piece), piece)
            fix = jnp.dot(table_ref[at], stacked, preferred_element_type=F32)
            cyc[p, r, at] = (cyc[p, r, at].astype(F32) + fix).astype(BF)
            return carry

        lax.fori_loop(0, length // piece, add, 0)

    for p in range(phases):
        whole(p, recv1).wait()

        def one(r, carry):
            filter_row(p, r)
            return carry

        lax.fori_loop(0, part, one, 0)
        each_peer(lambda pf, pt: back(p, pf, pt).start())
        back_self(p).start()

    @pl.when(tile < tiles - 1)
    def _():
        to_right().wait_send()

    @pl.when(tile > 0)
    def _():
        to_left().wait_send()

    for side, end, other in ends:
        @pl.when(tile == end)
        def _():
            seam_copy(face * 2 + side, 0, face, other).wait_send()
            for k in range(1, faces):
                pf = (face + k) % faces
                seam_copy(face * 2 + side, k, pf, end).wait_send()
                seam_copy(face * 2 + 1 - side, faces + k - 1, pf, end).wait_send()

    for p in range(phases):
        others(p, send1).wait()
    for p in range(phases):
        others(p, send2).wait()
        whole(p, recv2).wait()


def hand_on(src, dst, held, in_sem, out_sem):
    count = in_sem.shape[0]
    step = src.shape[0] // count
    pieces = [pl.ds(k * step, step) for k in range(count)]
    loads = [pltpu.make_async_copy(src.at[p], held.at[p], in_sem.at[k]) for k, p in enumerate(pieces)]
    stores = [pltpu.make_async_copy(held.at[p], dst.at[p], out_sem.at[k]) for k, p in enumerate(pieces)]
    for load in loads:
        load.start()
    for load, store in zip(loads, stores):
        load.wait()
        store.start()
    for store in stores:
        store.wait()


def per_device(faces, tiles, field, conv_weight, norm_gain, filter_gain, seam_face, seam_code):
    block_in = field[0]
    rows, width, chan = block_in.shape
    modes = filter_gain.shape[1]
    devices = faces * tiles
    length = devices * width
    owned = rows // devices
    phases = 2 if owned % 2 == 0 else 1
    part = owned // phases
    table = make_table(length, modes)
    group = rows // (2 * faces)
    anyw = pl.BlockSpec(memory_space=pl.ANY)
    vmem = pl.BlockSpec(memory_space=pltpu.VMEM)
    smem = pl.BlockSpec(memory_space=pltpu.SMEM)
    dma = pltpu.SemaphoreType.DMA
    out = pl.pallas_call(
        functools.partial(kernel, faces, tiles),
        out_shape=jax.ShapeDtypeStruct((rows, width, chan), BF),
        in_specs=[anyw] + [vmem] * 2 + [anyw] * 3 + [smem] * 2,
        out_specs=anyw,
        scratch_shapes=[
            pltpu.VMEM((rows, width, chan), BF),
            pltpu.VMEM((3, 3 * chan, chan), BF),
            pltpu.VMEM((length, 2 * modes), BF),
            pltpu.VMEM((2 * modes, length), BF),
            pltpu.VMEM((2, rows, chan), BF),
            pltpu.VMEM((2 * faces, rows, chan), BF),
            pltpu.VMEM((2, rows, chan), BF),
            pltpu.VMEM((2, rows, 1, chan), F32),
            pltpu.VMEM((group + 2, width, 3 * chan), BF),
            pltpu.VMEM((rows, width, chan), BF),
            pltpu.VMEM((phases, part, length, chan), BF),
            dma((2,)),
            dma((2,)),
            dma((2 * faces,)),
            dma((2 * faces,)),
            dma((phases,)),
            dma((phases,)),
            dma((phases,)),
            dma((phases,)),
            dma((4,)),
        ],
        compiler_params=pltpu.CompilerParams(
            collective_id=0, has_side_effects=True, vmem_limit_bytes=60 * 1024 * 1024
        ),
    )(
        block_in,
        norm_gain.reshape(1, chan),
        filter_gain,
        conv_weight.reshape(3, 3 * chan, chan),
        jnp.asarray(table),
        jnp.asarray(np.ascontiguousarray(table.T)),
        seam_face.T,
        seam_code.T,
    )
    done = pl.pallas_call(
        hand_on,
        out_shape=jax.ShapeDtypeStruct((rows, width, chan), BF),
        in_specs=[anyw],
        out_specs=anyw,
        scratch_shapes=[pltpu.VMEM((rows, width, chan), BF), dma((8,)), dma((8,))],
    )(out)
    return done[None]


def solution(mesh):
    placed = (P("face", None, "tile", None), P(), P(), P(), P(), P())
    return jax.shard_map(
        functools.partial(per_device, mesh.shape["face"], mesh.shape["tile"]),
        mesh=mesh,
        in_specs=placed,
        out_specs=P("face", None, "tile", None),
        check_vma=False,
    )
```

```python
import functools

import jax
import jax.numpy as jnp
import numpy as np
from jax import lax
from jax.experimental import pallas as pl
from jax.experimental.pallas import tpu as pltpu
from jax.sharding import PartitionSpec as P

MESH = pl.DeviceIdType.MESH
BF = jnp.bfloat16
F32 = jnp.float32


def make_table(length, modes):
    phase = np.arange(length)[:, None] * np.arange(modes)[None, :] % length
    angle = phase.astype(np.float64) * (2.0 * np.pi / length)
    return np.concatenate([np.cos(angle), np.sin(angle)], axis=1).astype(BF)


def kernel(
    faces,
    tiles,
    x_hbm,
    gain_ref,
    fgain_ref,
    w_hbm,
    table_hbm,
    tablet_hbm,
    sface_ref,
    scode_ref,
    out_ref,
    x_ref,
    w_ref,
    table_ref,
    tablet_ref,
    edge_ref,
    seam,
    near,
    halo,
    x3,
    mixed,
    cyc,
    near_send,
    near_recv,
    seam_send,
    seam_recv,
    send1,
    recv1,
    send2,
    recv2,
    load_sem,
):
    rows, width, chan = x_hbm.shape
    devices = faces * tiles
    owned = rows // devices
    phases, part = cyc.shape[0], cyc.shape[1]
    length = devices * width
    modes = fgain_ref.shape[1]
    half = tiles // 2
    group = half * owned
    face = lax.axis_index("face")
    tile = lax.axis_index("tile")
    me = face * tiles + tile

    barrier = pltpu.get_barrier_semaphore()

    loads = [
        pltpu.make_async_copy(src, dst, load_sem.at[k])
        for k, (src, dst) in enumerate(
            ((x_hbm, x_ref), (w_hbm, w_ref), (tablet_hbm, tablet_ref), (table_hbm, table_ref))
        )
    ]
    loads[0].start()

    def peer(k):
        side = k // (faces * half)
        rest = k % (faces * half)
        pf = (face + rest // half) % faces
        pt = ((tile // half + 1 + side) % 2) * half + (tile % half + rest % half) % half
        return pf, pt

    own = devices // 2

    def each_peer(fn):
        def step(k, carry):
            @pl.when(k != own)
            def _():
                pf, pt = peer(k)
                fn(pf, pt)

            return carry

        lax.fori_loop(0, devices, step, 0)

    each_peer(
        lambda pf, pt: pl.semaphore_signal(barrier, inc=1, device_id=(pf, pt), device_id_type=MESH)
    )
    def pick(b, carry):
        at = pl.ds(b * 16, 16)
        edge_ref[0, at] = x_ref[at, 0:16].astype(F32)[:, 0, :].astype(BF)
        edge_ref[1, at] = x_ref[at, width - 16 : width].astype(F32)[:, 15, :].astype(BF)
        return carry

    loads[0].wait()
    for load in loads[1:]:
        load.start()
    lax.fori_loop(0, rows // 16, pick, 0)
    pl.semaphore_wait(barrier, devices - 1)

    def to_right():
        return pltpu.make_async_remote_copy(
            edge_ref.at[1], near.at[0], near_send.at[0], near_recv.at[0],
            device_id=(face, (tile + 1) % tiles), device_id_type=MESH,
        )

    def to_left():
        return pltpu.make_async_remote_copy(
            edge_ref.at[0], near.at[1], near_send.at[1], near_recv.at[1],
            device_id=(face, (tile + tiles - 1) % tiles), device_id_type=MESH,
        )

    def seam_copy(slot, k, pf, pt):
        return pltpu.make_async_remote_copy(
            seam.at[slot], seam.at[slot], seam_send.at[k], seam_recv.at[slot],
            device_id=(pf, pt), device_id_type=MESH,
        )

    ends = ((0, 0, tiles - 1), (1, tiles - 1, 0))

    @pl.when(tile < tiles - 1)
    def _():
        to_right().start()

    @pl.when(tile > 0)
    def _():
        to_left().start()

    for side, end, other in ends:
        @pl.when(tile == end)
        def _():
            mine = face * 2 + side
            seam[mine] = edge_ref[side]
            seam_copy(mine, 0, face, other).start()
            for k in range(1, faces):
                seam_copy(mine, k, (face + k) % faces, end).start()

    @pl.when(tile > 0)
    def _():
        to_right().wait_recv()
        halo[0] = near[0].astype(F32).reshape(rows, 1, chan)

    @pl.when(tile < tiles - 1)
    def _():
        to_left().wait_recv()
        halo[1] = near[1].astype(F32).reshape(rows, 1, chan)

    down = lax.broadcasted_iota(jnp.int32, (rows, rows), 0)
    across = lax.broadcasted_iota(jnp.int32, (rows, rows), 1)
    for side, end, other in ends:
        @pl.when(tile == end)
        def _():
            far = face * 2 + 1 - side
            seam_copy(far, 0, face, other).wait_recv()
            for k in range(1, faces):
                seam_copy(far, faces + k - 1, (face + k) % faces, end).start()
            for k in range(1, faces):
                pf = (face + k) % faces
                seam_copy(pf * 2 + side, k, pf, end).wait_recv()
                seam_copy(pf * 2 + 1 - side, faces + k - 1, pf, end).wait_recv()
            code = scode_ref[side, face]
            strip = seam[sface_ref[side, face] * 2 + code % 2]
            target = jnp.where(code >= 2, rows - 1 - down, down)
            order = jnp.where(target == across, 1.0, 0.0).astype(BF)
            halo[side] = jnp.dot(order, strip, preferred_element_type=F32).reshape(rows, 1, chan)

    def shift(dst, row, count):
        at = pl.ds(row, count)
        here = x_ref[at]
        wide = here.astype(F32)
        col = lax.broadcasted_iota(jnp.int32, wide.shape, 1)
        x3[dst, :, 0:chan] = jnp.where(col == 0, halo[0, at], pltpu.roll(wide, 1, 1)).astype(BF)
        x3[dst, :, chan : 2 * chan] = here
        x3[dst, :, 2 * chan : 3 * chan] = jnp.where(
            col == width - 1, halo[1, at], pltpu.roll(wide, width - 1, 1)
        ).astype(BF)

    def frame(base):
        batch = 8 if group % 8 == 0 else group
        for b in range(0, group, batch):
            shift(pl.ds(b + 1, batch), base + b, batch)
        for dst, row, edge in ((0, base - 1, 0), (group + 1, base + group, rows - group)):
            @pl.when(base != edge)
            def _():
                shift(pl.ds(dst, 1), row, 1)

            @pl.when(base == edge)
            def _():
                x3[dst] = jnp.zeros(x3.shape[1:], BF)

    loads[1].wait()

    def forward(p, pf, pt):
        d = pf * tiles + pt
        return pltpu.make_async_remote_copy(
            mixed.at[pl.ds(d * owned + p * part, part)],
            cyc.at[p, :, pl.ds(me * width, width), :],
            send1.at[p],
            recv1.at[p],
            device_id=(pf, pt),
            device_id_type=MESH,
        )

    def forward_self(p):
        return pltpu.make_async_copy(
            mixed.at[pl.ds(me * owned + p * part, part)],
            cyc.at[p, :, pl.ds(me * width, width), :],
            recv1.at[p],
        )

    def whole(p, sem):
        return pltpu.make_async_copy(mixed.at[pl.ds(0, devices * part)], mixed.at[pl.ds(0, devices * part)], sem.at[p])

    def others(p, sem):
        return pltpu.make_async_copy(
            mixed.at[pl.ds(0, (devices - 1) * part)], mixed.at[pl.ds(0, (devices - 1) * part)], sem.at[p]
        )

    gain = gain_ref[...]

    def block(g, carry):
        side = g // faces
        pf = (face + g % faces) % faces
        ph = (tile // half + 1 + side) % 2
        base = (pf * tiles + ph * half) * owned
        frame(base)
        total = jnp.zeros((group * width, chan), F32)
        for dy in range(3):
            total += jnp.dot(
                x3[pl.ds(dy, group)].reshape(group * width, 3 * chan),
                w_ref[dy],
                preferred_element_type=F32,
            )
        step = group // 4 if group % 4 == 0 else group
        for q in range(group // step):
            piece = total[q * step * width : (q + 1) * step * width]
            centered = piece - jnp.mean(piece, axis=1, keepdims=True)
            variance = jnp.mean(centered * centered, axis=1, keepdims=True)
            normed = centered * (lax.rsqrt(variance + 1e-05)) * gain
            inner = normed * (0.7978845608028654 + 0.035677408136300125 * (normed * normed))
            act = 0.5 * normed * (1.0 + jnp.tanh(inner))
            src = x_ref[pl.ds(base + q * step, step)].astype(F32)
            mixed[pl.ds(base + q * step, step)] = (src + act.reshape(step, width, chan)).astype(BF)

        def push(i, inner_carry):
            pt = ph * half + (tile % half + i) % half

            @pl.when(g * half + i != own)
            def _():
                forward(0, pf, pt).start()

            return inner_carry

        lax.fori_loop(0, half, push, 0)
        return carry

    lax.fori_loop(0, 2 * faces, block, 0)
    for p in range(phases):
        forward_self(p).start()
    for p in range(1, phases):
        others(p - 1, send1).wait()
        each_peer(lambda pf, pt: forward(p, pf, pt).start())

    def back(p, pf, pt):
        d = pf * tiles + pt
        return pltpu.make_async_remote_copy(
            cyc.at[p, :, pl.ds(d * width, width), :],
            out_ref.at[pl.ds(me * owned + p * part, part)],
            send2.at[p],
            recv2.at[p],
            device_id=(pf, pt),
            device_id_type=MESH,
        )

    def back_self(p):
        return pltpu.make_async_copy(
            cyc.at[p, :, pl.ds(me * width, width), :],
            out_ref.at[pl.ds(me * owned + p * part, part)],
            recv2.at[p],
        )

    loads[2].wait()
    loads[3].wait()
    width_m = min(modes, 256)
    eye = lax.broadcasted_iota(jnp.int32, (width_m, width_m), 0) == lax.broadcasted_iota(
        jnp.int32, (width_m, width_m), 1
    )
    stand = lambda row: jnp.sum(jnp.where(eye, row, 0.0), axis=1, keepdims=True)

    def filter_row(p, r):
        held = []
        for start in range(0, modes, width_m):
            waves = start + lax.broadcasted_iota(jnp.int32, (width_m, 1), 0)
            scale = jnp.where(waves == 0, 1.0 / length, 2.0 / length)
            real_gain = stand(fgain_ref[0:1, start : start + width_m]) * scale
            imag_gain = stand(fgain_ref[1:2, start : start + width_m]) * scale
            line = cyc[p, r]
            cos_part = jnp.dot(tablet_ref[start : start + width_m], line, preferred_element_type=F32)
            sin_part = jnp.dot(
                tablet_ref[modes + start : modes + start + width_m], line, preferred_element_type=F32
            )
            held.append(
                (
                    (real_gain * cos_part + imag_gain * sin_part).astype(BF),
                    (real_gain * sin_part - imag_gain * cos_part).astype(BF),
                )
            )
        stacked = jnp.concatenate([h[0] for h in held] + [h[1] for h in held], axis=0)
        piece = 256

        def add(b, carry):
            at = pl.ds(pl.multiple_of(b * piece, piece), piece)
            fix = jnp.dot(table_ref[at], stacked, preferred_element_type=F32)
            cyc[p, r, at] = (cyc[p, r, at].astype(F32) + fix).astype(BF)
            return carry

        lax.fori_loop(0, length // piece, add, 0)

    for p in range(phases):
        whole(p, recv1).wait()

        def one(r, carry):
            filter_row(p, r)
            return carry

        lax.fori_loop(0, part, one, 0)
        each_peer(lambda pf, pt: back(p, pf, pt).start())
        back_self(p).start()

    @pl.when(tile < tiles - 1)
    def _():
        to_right().wait_send()

    @pl.when(tile > 0)
    def _():
        to_left().wait_send()

    for side, end, other in ends:
        @pl.when(tile == end)
        def _():
            seam_copy(face * 2 + side, 0, face, other).wait_send()
            for k in range(1, faces):
                pf = (face + k) % faces
                seam_copy(face * 2 + side, k, pf, end).wait_send()
                seam_copy(face * 2 + 1 - side, faces + k - 1, pf, end).wait_send()

    others(phases - 1, send1).wait()
    for p in range(phases):
        others(p, send2).wait()
        whole(p, recv2).wait()


def hand_on(src, dst, held, in_sem, out_sem):
    count = in_sem.shape[0]
    step = src.shape[0] // count
    pieces = [pl.ds(k * step, step) for k in range(count)]
    loads = [pltpu.make_async_copy(src.at[p], held.at[p], in_sem.at[k]) for k, p in enumerate(pieces)]
    stores = [pltpu.make_async_copy(held.at[p], dst.at[p], out_sem.at[k]) for k, p in enumerate(pieces)]
    for load in loads:
        load.start()
    for load, store in zip(loads, stores):
        load.wait()
        store.start()
    for store in stores:
        store.wait()


def per_device(faces, tiles, field, conv_weight, norm_gain, filter_gain, seam_face, seam_code):
    block_in = field[0]
    rows, width, chan = block_in.shape
    modes = filter_gain.shape[1]
    devices = faces * tiles
    length = devices * width
    owned = rows // devices
    phases = 2 if owned % 2 == 0 else 1
    part = owned // phases
    table = make_table(length, modes)
    group = rows // (2 * faces)
    anyw = pl.BlockSpec(memory_space=pl.ANY)
    vmem = pl.BlockSpec(memory_space=pltpu.VMEM)
    smem = pl.BlockSpec(memory_space=pltpu.SMEM)
    dma = pltpu.SemaphoreType.DMA
    out = pl.pallas_call(
        functools.partial(kernel, faces, tiles),
        out_shape=jax.ShapeDtypeStruct((rows, width, chan), BF),
        in_specs=[anyw] + [vmem] * 2 + [anyw] * 3 + [smem] * 2,
        out_specs=anyw,
        scratch_shapes=[
            pltpu.VMEM((rows, width, chan), BF),
            pltpu.VMEM((3, 3 * chan, chan), BF),
            pltpu.VMEM((length, 2 * modes), BF),
            pltpu.VMEM((2 * modes, length), BF),
            pltpu.VMEM((2, rows, chan), BF),
            pltpu.VMEM((2 * faces, rows, chan), BF),
            pltpu.VMEM((2, rows, chan), BF),
            pltpu.VMEM((2, rows, 1, chan), F32),
            pltpu.VMEM((group + 2, width, 3 * chan), BF),
            pltpu.VMEM((rows, width, chan), BF),
            pltpu.VMEM((phases, part, length, chan), BF),
            dma((2,)),
            dma((2,)),
            dma((2 * faces,)),
            dma((2 * faces,)),
            dma((phases,)),
            dma((phases,)),
            dma((phases,)),
            dma((phases,)),
            dma((4,)),
        ],
        compiler_params=pltpu.CompilerParams(
            collective_id=0, has_side_effects=True, vmem_limit_bytes=60 * 1024 * 1024
        ),
    )(
        block_in,
        norm_gain.reshape(1, chan),
        filter_gain,
        conv_weight.reshape(3, 3 * chan, chan),
        jnp.asarray(table),
        jnp.asarray(np.ascontiguousarray(table.T)),
        seam_face.T,
        seam_code.T,
    )
    done = pl.pallas_call(
        hand_on,
        out_shape=jax.ShapeDtypeStruct((rows, width, chan), BF),
        in_specs=[anyw],
        out_specs=anyw,
        scratch_shapes=[pltpu.VMEM((rows, width, chan), BF), dma((8,)), dma((8,))],
    )(out)
    return done[None]


def solution(mesh):
    placed = (P("face", None, "tile", None), P(), P(), P(), P(), P())
    return jax.shard_map(
        functools.partial(per_device, mesh.shape["face"], mesh.shape["tile"]),
        mesh=mesh,
        in_specs=placed,
        out_specs=P("face", None, "tile", None),
        check_vma=False,
    )
```
